256 devices in a mesh: dp: 8 (over x_hi, y), vocab: 16 (over z, core), pair: 2 (over x_lo).
Axes of the slice: x: 4 (x_hi: 2, x_lo: 2; x = x_hi * 2 + x_lo), y: 4, z: 8, core: 2. Of those that a mesh axis runs over, the one named last changes fastest.
Arguments:
- teacher_hidden: bfloat16 [1024, 4096], P('dp')
- student_hidden: bfloat16 [1024, 4096], P('dp')
- layer_input: bfloat16 [1024, 4096], P('dp'), may hold values from -6 to 6
- head: bfloat16 [2, 81920, 4096], P('pair', ('dp', 'vocab'))
- teacher_gain: bfloat16 [4096], replicated, may hold values from 0.5 to 1.5
- student_gain: bfloat16 [4096], replicated, may hold values from 0.5 to 1.5
- mlp_gain: bfloat16 [4096], replicated, may hold values from 0.5 to 1.5
- w_gate: bfloat16 [4096, 12288], P(None, ('dp', 'vocab', 'pair')), may hold values from -0.09375 to 0.09375
- w_up: bfloat16 [4096, 12288], P(None, ('dp', 'vocab', 'pair')), may hold values from -0.09375 to 0.09375
- w_down: bfloat16 [12288, 4096], P(('dp', 'vocab', 'pair')), may hold values from -0.0546875 to 0.0546875
- positions: int32 [8, 64], P('dp'), may hold values from 0 to 127, as said below
- verified: int32 [8, 64], replicated, may hold values 0 or 1
Outputs:
- d_head: bfloat16 [81920, 4096], P(('dp', 'vocab'), 'pair')
- d_gate: bfloat16 [4096, 12288], P(None, ('dp', 'vocab', 'pair'))
- d_up: bfloat16 [4096, 12288], P(None, ('dp', 'vocab', 'pair'))
- d_down: bfloat16 [12288, 4096], P(('dp', 'vocab', 'pair'))
The draws below stay inside these ranges and needn't reach their ends.
Inputs may be any that keep to these rules, and one draw needn't show every extreme that they name: positions within one block are distinct.
All inputs are finite; a program needn't handle non-finite values.
Results may differ from the reference program's by a relative error of at most 0.015.
The reference program's roundings to bfloat16 on the way (of `grad_logits`, `d_final` and `hidden_act`) count: a program that leaves them out, or rounds other values in their place, can miss the bound.
Values may be sent and summed in bfloat16 or wider, within the bound.
No kernel may reach another device: no remote copies, remote signals or barrier semaphores. Data moves between devices by JAX's collectives and lax.ppermute only.
A program may use at most 128 MiB of HBM per device.

```python
import math
import jax
import jax.numpy as jnp
from jax import lax

D = 4096
FF = 12288
VOCAB = 81920
BLOCK = 128
MASK_BLK = 64
BLOCKS = 8
TOKENS = 1024


def rolled(shuffle, target):
    offset = jnp.argmax(shuffle == target)
    return jnp.roll(shuffle, -offset)


def positions_table(key):
    table_key = jax.random.fold_in(key, 101)
    block_keys = jax.random.split(table_key, BLOCKS)
    shuffled = jax.vmap(lambda block_key: jax.random.permutation(block_key, BLOCK))(block_keys).astype(jnp.int32)
    shuffled = shuffled.at[0].set(rolled(shuffled[0], BLOCK - 1))
    shuffled = shuffled.at[1].set(rolled(shuffled[1], 0))
    return shuffled[:, :MASK_BLK].astype(jnp.int32)


def hidden_base(key):
    first_key, second_key = jax.random.split(key)
    base_draw = jax.random.normal(first_key, (TOKENS, D), jnp.float32)
    row_scale = jnp.exp(jax.random.uniform(second_key, (TOKENS, 1), jnp.float32, 0.0, math.log(10.0)))
    return base_draw * row_scale


def draw_positions(key, part):
    table = positions_table(key)
    return table


def draw_teacher_hidden(key, part):
    key = jax.random.fold_in(key, 2)
    hidden = hidden_base(key)
    return hidden.astype(jnp.bfloat16)


def draw_student_hidden(key, part):
    key = jax.random.fold_in(key, 3)
    hidden = hidden_base(key)
    return hidden.astype(jnp.bfloat16)


def draw_head(key, part):
    key = jax.random.fold_in(key, 4)
    first_key, second_key = jax.random.split(key, 2)
    row_scale = jnp.exp(jax.random.uniform(second_key, (2, VOCAB, 1), jnp.float32, math.log(0.6), math.log(6.0)))
    weights = jax.random.normal(first_key, (2, VOCAB, D), jnp.float32) * row_scale / math.sqrt(D)
    return weights.astype(jnp.bfloat16)


def with_ends(entries, stream_key, low, top_value):
    longest = entries.shape.index(max(entries.shape))
    spots = []
    for shift in (0, 1):
        where = [jax.random.randint(jax.random.fold_in(stream_key, axis), (), 0, length) for axis, length in enumerate(entries.shape)]
        where[longest] = (where[longest] + shift) % entries.shape[longest]
        spots.append(tuple(where))
    return entries.at[spots[0]].set(low).at[spots[1]].set(top_value)


def level_of(own_key, shape, cuts, low, high):
    loudness = 1.0
    for dim, shards_of in cuts:
        steps = jax.random.uniform(jax.random.fold_in(jax.random.fold_in(own_key, 6), dim), (shards_of,), jnp.float32, low / len(cuts), high / len(cuts))
        loudness = loudness * jnp.repeat(jnp.exp(steps), shape[dim] // shards_of).reshape((-1,) + (1,) * (len(shape) - 1 - dim))
    return loudness


def scatter_about(own_key, dims, deviation, limit, pieces=(), held_as=jnp.bfloat16):
    values = jax.random.normal(own_key, dims, jnp.float32) * deviation
    if len(pieces) > 0:
        values = level_of(own_key, dims, pieces, -0.22, 0.18) * values
    return jnp.clip(values, min=-limit, max=limit).astype(held_as)


def setup_inputs(seed: int = 0) -> dict:
    streams_of = jax.random.split(jax.random.key(seed), 13)
    return {
        "teacher_hidden": draw_teacher_hidden(jax.random.fold_in(streams_of[12], 71), 0),
        "student_hidden": draw_student_hidden(jax.random.fold_in(streams_of[12], 71), 0),
        "layer_input": scatter_about(streams_of[2], (TOKENS, D), 1.0, 6.0, ((0, 8),)),
        "head": draw_head(jax.random.fold_in(streams_of[12], 71), 0),
        "teacher_gain": jnp.clip(1.0 + 0.1 * jax.random.normal(streams_of[4], (D,), jnp.float32), 0.5, 1.5).astype(jnp.bfloat16),
        "student_gain": jnp.clip(1.0 + 0.1 * jax.random.normal(streams_of[5], (D,), jnp.float32), 0.5, 1.5).astype(jnp.bfloat16),
        "mlp_gain": jnp.clip(1.0 + 0.1 * jax.random.normal(streams_of[6], (D,), jnp.float32), 0.5, 1.5).astype(jnp.bfloat16),
        "w_gate": scatter_about(streams_of[7], (D, FF), D ** -0.5, 0.09375, ((1, 256),)),
        "w_up": scatter_about(streams_of[8], (D, FF), D ** -0.5, 0.09375, ((1, 256),)),
        "w_down": scatter_about(streams_of[9], (FF, D), FF ** -0.5, 0.0546875, ((0, 256),)),
        "positions": draw_positions(jax.random.fold_in(streams_of[12], 71), 0),
        "verified": with_ends((jax.random.randint(streams_of[11], (BLOCKS, MASK_BLK), 0, 4) < 3).astype(jnp.int32), jax.random.fold_in(streams_of[11], 1), 0, 1),
    }


loss_scale = 256.0
norm_eps = 1e-05

def rms_scale(values):
    return lax.rsqrt(lax.optimization_barrier(jnp.mean(values * values, axis=-1, keepdims=True)) + norm_eps)

def normalize(hidden, gain_vector):
    widened = hidden.astype(jnp.float32)
    return (widened * rms_scale(widened) * gain_vector.astype(jnp.float32)).astype(jnp.bfloat16)

def norm_back(hidden, upstream, gain_vector):
    widened = hidden.astype(jnp.float32)
    factor = rms_scale(widened)
    scaled = upstream * gain_vector.astype(jnp.float32)
    inner_sum = lax.optimization_barrier(jnp.mean(scaled * widened, axis=-1, keepdims=True))
    return (factor * scaled - widened * factor * factor * factor * inner_sum).astype(jnp.bfloat16)

def softmax_rows(logits):
    widened = logits.astype(jnp.float32)
    exp_terms = jnp.exp(widened - lax.optimization_barrier(jnp.max(widened, axis=1, keepdims=True)))
    return exp_terms / lax.optimization_barrier(jnp.sum(exp_terms, axis=1, keepdims=True))

def reference(teacher_hidden, student_hidden, layer_input, head, teacher_gain, student_gain, mlp_gain, w_gate, w_up, w_down, positions, verified):
    starts = (jnp.arange(BLOCKS, dtype=jnp.int32) * BLOCK)[:, None]
    picked = (starts + positions).reshape(-1).astype(jnp.int32)
    rows_teacher = teacher_hidden[picked]
    rows_student = student_hidden[picked]
    rows_input = layer_input[picked]
    normed_teacher = normalize(rows_teacher, teacher_gain)
    normed_student = normalize(rows_student, student_gain)
    logits_teacher = jnp.dot(normed_teacher, head[0].T, preferred_element_type=jnp.float32).astype(jnp.bfloat16)
    logits_student = jnp.dot(normed_student, head[1].T, preferred_element_type=jnp.float32).astype(jnp.bfloat16)
    probs_teacher = softmax_rows(logits_teacher)
    probs_student = softmax_rows(logits_student)
    weights_row = verified.reshape(-1).astype(jnp.float32)[:, None]
    grad_logits = (loss_scale * weights_row * (probs_student - probs_teacher)).astype(jnp.bfloat16)
    d_head = jnp.dot(grad_logits.T, normed_student, preferred_element_type=jnp.float32).astype(jnp.bfloat16)
    d_normed = jnp.dot(grad_logits, head[1], preferred_element_type=jnp.float32)
    d_final = norm_back(rows_student, d_normed, student_gain)
    normed_input = normalize(rows_input, mlp_gain)
    gate_pre = jnp.dot(normed_input, w_gate, preferred_element_type=jnp.float32)
    up_pre = jnp.dot(normed_input, w_up, preferred_element_type=jnp.float32)
    gate_sigmoid = jax.nn.sigmoid(gate_pre)
    hidden_act = (gate_pre * gate_sigmoid * up_pre).astype(jnp.bfloat16)
    d_act = jnp.dot(d_final, w_down.T, preferred_element_type=jnp.float32)
    d_gate_pre = (d_act * up_pre * gate_sigmoid * (1.0 + gate_pre * (1.0 - gate_sigmoid))).astype(jnp.bfloat16)
    d_up_pre = (d_act * gate_pre * gate_sigmoid).astype(jnp.bfloat16)
    d_gate = jnp.dot(normed_input.T, d_gate_pre, preferred_element_type=jnp.float32).astype(jnp.bfloat16)
    d_up = jnp.dot(normed_input.T, d_up_pre, preferred_element_type=jnp.float32).astype(jnp.bfloat16)
    d_down = jnp.dot(hidden_act.T, d_final, preferred_element_type=jnp.float32).astype(jnp.bfloat16)
    return (d_head, d_gate, d_up, d_down)
```

```python
import jax
import jax.numpy as jnp
from jax import lax
from jax.sharding import PartitionSpec as P

loss_scale = 256.0
norm_eps = 1e-05
mesh_axes = ("dp", "vocab", "pair")

gray = (0, 1, 3, 2)


def moved(block, target, senders=None):
    route = []
    for x in range(4):
        if senders is not None and x not in senders:
            continue
        for y in range(4):
            for z in range(8):
                for c in range(2):
                    tx, ty, tz, tc = target(x, y, z, c)
                    here = (((x // 2) * 4 + y) * 16 + z * 2 + c) * 2 + x % 2
                    there = (((tx // 2) * 4 + ty) * 16 + tz * 2 + tc) * 2 + tx % 2
                    route.append((here, there))
    return lax.ppermute(block, mesh_axes, route)


def along_y(block, distance):
    return moved(block, lambda x, y, z, c: (x, gray[gray[y] ^ distance], z, c))


def along_z(block, distance):
    return moved(block, lambda x, y, z, c: (x, y, z ^ distance, c))


def to_pair(block, senders=None):
    return moved(block, lambda x, y, z, c: (x ^ 1, y, z, c), senders)


def to_outer(block, senders=None):
    return moved(block, lambda x, y, z, c: (3 - x, y, z, c), senders)


def to_opposite(block, senders=None):
    return moved(block, lambda x, y, z, c: (x ^ 2, y, z, c), senders)


def to_core(block):
    return moved(block, lambda x, y, z, c: (x, y, z, c ^ 1))


def after(block, *others):
    return lax.optimization_barrier((block, *others))[0]


def rms_scale(values):
    return lax.rsqrt(jnp.mean(values * values, axis=-1, keepdims=True) + norm_eps)


def normalize(hidden, gain_vector):
    widened = hidden.astype(jnp.float32)
    return (widened * rms_scale(widened) * gain_vector.astype(jnp.float32)).astype(jnp.bfloat16)


def norm_back(hidden, upstream, gain_vector):
    widened = hidden.astype(jnp.float32)
    factor = rms_scale(widened)
    scaled = upstream * gain_vector.astype(jnp.float32)
    inner_sum = jnp.mean(scaled * widened, axis=-1, keepdims=True)
    return (factor * scaled - widened * factor * factor * factor * inner_sum).astype(jnp.bfloat16)


def gathered(own, outer, swap):
    near = [along_y(own, 1), along_y(own, 2)]
    near_outer = [along_y(outer, 1), along_y(outer, 2)]
    half = own.shape[0] // 2
    far = jnp.concatenate([along_y(near[0][:half], 2), along_y(near[1][half:], 1)])
    far_outer = jnp.concatenate([along_y(near_outer[0][:half], 2), along_y(near_outer[1][half:], 1)])
    pieces = []
    for mine, others in ((own, outer), (near[0], near_outer[0]), (near[1], near_outer[1]), (far, far_outer)):
        pieces += [jnp.where(swap, others, mine), jnp.where(swap, mine, others)]
    return jnp.concatenate(pieces)


def merge(peaks, totals):
    peak = jnp.max(jnp.stack(peaks), axis=0)
    total = sum(t * jnp.exp(p - peak) for p, t in zip(peaks, totals))
    return peak, total


def shards(
    teacher_hidden,
    student_hidden,
    layer_input,
    head,
    teacher_gain,
    student_gain,
    mlp_gain,
    w_gate,
    w_up,
    w_down,
    positions,
    verified,
):
    f32 = jnp.float32
    bf16 = jnp.bfloat16
    dp, vocab = lax.axis_index("dp"), lax.axis_index("vocab")
    is_student = lax.axis_index("pair") == 1
    x_hi, y, z, c = dp // 4, dp % 4, vocab // 2, vocab % 2
    g = y ^ (y >> 1)
    swap = x_hi != (z >> 2)
    width = head.shape[2]
    mask_blk = positions.shape[1]
    half_blk = mask_blk // 2
    group = half_blk // 4
    rows = 8 * half_blk

    head_own = head[0]
    head_other = to_core(head_own)

    step = jnp.arange(half_blk, dtype=jnp.int32)
    order = c * half_blk + ((step // group) ^ (z & 3)) * group + step % group
    picked = positions[0][order]
    raw_teacher, raw_student, raw_input = (
        teacher_hidden[picked],
        student_hidden[picked],
        layer_input[picked],
    )
    own_teacher = normalize(raw_teacher, teacher_gain)
    own_student = normalize(raw_student, student_gain)
    own_rows = jnp.where(is_student, own_student, own_teacher)
    send_rows = jnp.where(is_student, own_teacher, own_student)
    outer_rows = to_outer(send_rows)
    normed = gathered(own_rows, outer_rows, swap)

    contract_width = (((1,), (1,)), ((), ()))
    contract_rows = (((0,), (0,)), ((), ()))
    logits_own = lax.dot_general(
        normed, head_own, contract_width, preferred_element_type=f32
    ).astype(bf16)
    partner_own = to_pair(logits_own)
    logits_side = lax.dot_general(
        normed, head_other, contract_width, preferred_element_type=f32
    ).astype(bf16)
    partner_side = to_pair(logits_side)

    wide_own, wide_side = logits_own.astype(f32), logits_side.astype(f32)
    peak_here = jnp.maximum(
        jnp.max(wide_own, axis=1, keepdims=True), jnp.max(wide_side, axis=1, keepdims=True)
    )
    total_here = jnp.sum(jnp.exp(wide_own - peak_here), axis=1, keepdims=True) + jnp.sum(
        jnp.exp(wide_side - peak_here), axis=1, keepdims=True
    )
    flips = (g * 8 + z) * group
    row_ids = lax.broadcasted_iota(jnp.int32, (rows, rows), 0)
    col_ids = lax.broadcasted_iota(jnp.int32, (rows, rows), 1)
    same_row = (row_ids ^ flips) == col_ids

    def absolute(column):
        return jnp.sum(jnp.where(same_row, column, 0.0), axis=0)

    def relative(line):
        return jnp.sum(jnp.where(same_row, line[None, :], 0.0), axis=1, keepdims=True)

    stats = jnp.stack([absolute(peak_here), absolute(total_here)])
    parts = [stats] + [along_z(stats, q) for q in range(1, 8)]
    stats = jnp.stack(merge([p[0] for p in parts], [p[1] for p in parts]))
    parts = [stats] + [along_y(stats, d) for d in range(1, 4)]
    stats = jnp.stack(merge([p[0] for p in parts], [p[1] for p in parts]))
    opposite, pair_side, outer_side = to_opposite(stats), to_pair(stats), to_outer(stats)
    peak_mine, total_mine = merge([stats[0], opposite[0]], [stats[1], opposite[1]])
    peak_theirs, total_theirs = merge(
        [pair_side[0], outer_side[0]], [pair_side[1], outer_side[1]]
    )

    flags = verified.astype(f32).reshape(2, 4, 2, half_blk)
    flags = lax.dynamic_index_in_dim(flags, c, 2, keepdims=False)
    flags = jnp.stack([flags[:, gray[i]] for i in range(4)]).reshape(rows)
    sign = jnp.where(is_student, loss_scale, -loss_scale)
    scale = relative(flags * sign)
    peak_mine, total_mine = relative(peak_mine), relative(total_mine)
    peak_theirs, total_theirs = relative(peak_theirs), relative(total_theirs)

    def gradient(mine, theirs):
        probs_mine = jnp.exp(mine.astype(f32) - peak_mine) / total_mine
        probs_theirs = jnp.exp(theirs.astype(f32) - peak_theirs) / total_theirs
        return (scale * (probs_mine - probs_theirs)).astype(bf16)

    grad_own = gradient(logits_own, partner_own)
    grad_side = gradient(logits_side, partner_side)

    partial = jnp.dot(grad_own, head_own, preferred_element_type=f32) + jnp.dot(
        grad_side, head_other, preferred_element_type=f32
    )
    partial = partial.reshape(4, 2, half_blk, width)
    near = along_y(jnp.stack([partial[1, 0], partial[3, 0]]).astype(bf16), 1).astype(f32)
    cross = along_y(jnp.stack([partial[2, 1], partial[3, 1]]).astype(bf16), 2).astype(f32)
    near_next = along_y((partial[2, 0] + near[1]).astype(bf16), 2).astype(f32)
    cross_next = along_y((partial[1, 1] + cross[1]).astype(bf16), 1).astype(f32)
    first = (partial[0, 0] + near[0] + near_next).reshape(4, group, width)
    second = (partial[0, 1] + cross[0] + cross_next).reshape(4, group, width)
    chunks = [first[i] for i in range(4)] + [second[i] for i in range(4)]
    summed = chunks[0]
    for q in range(1, 8):
        summed = summed + along_z(chunks[q].astype(bf16), q).astype(f32)
    students = (1, 3)
    d_normed = (
        jnp.where(is_student, summed, 0.0)
        + to_opposite(summed, students)
        + to_pair(summed, students)
        + to_outer(summed, students)
    )
    raw_here = jnp.where(swap, to_outer(raw_student[:group]), raw_student[:group])
    d_chunk = norm_back(raw_here, d_normed, student_gain)
    d_local = jnp.concatenate([d_chunk] + [along_z(d_chunk, q) for q in range(1, 8)])
    d_near, d_cross = along_y(d_local, 1), along_y(d_local, 2)
    d_far = jnp.concatenate([along_y(d_near[:half_blk], 2), along_y(d_cross[half_blk:], 1)])
    d_pieces = [d_local, d_near, d_cross, d_far]
    d_final = jnp.concatenate(d_pieces + [to_core(piece) for piece in d_pieces])

    raw_after = after(normalize(raw_input, mlp_gain), normed)
    input_rows = gathered(raw_after, to_outer(raw_after), swap)
    normed_input = jnp.concatenate([input_rows, to_core(input_rows)])
    gate_pre = jnp.dot(normed_input, w_gate, preferred_element_type=f32)
    up_pre = jnp.dot(normed_input, w_up, preferred_element_type=f32)
    gate_sigmoid = jax.nn.sigmoid(gate_pre)
    hidden_act = (gate_pre * gate_sigmoid * up_pre).astype(bf16)

    half_width = width // 2
    lent = to_pair(after(normed, partner_side)[:, :half_width], students)
    columns = jnp.where(is_student, normed[:, half_width:], lent)
    columns = jnp.concatenate([columns, to_core(columns)])
    grad_all = jnp.concatenate([grad_own, to_core(grad_side)])
    d_head = lax.dot_general(
        grad_all, columns, contract_rows, preferred_element_type=f32
    ).astype(bf16)

    d_act = lax.dot_general(d_final, w_down, contract_width, preferred_element_type=f32)
    d_gate_pre = (d_act * up_pre * gate_sigmoid * (1.0 + gate_pre * (1.0 - gate_sigmoid))).astype(bf16)
    d_up_pre = (d_act * gate_pre * gate_sigmoid).astype(bf16)
    d_gate = lax.dot_general(
        normed_input, d_gate_pre, contract_rows, preferred_element_type=f32
    ).astype(bf16)
    d_up = lax.dot_general(
        normed_input, d_up_pre, contract_rows, preferred_element_type=f32
    ).astype(bf16)
    d_down = lax.dot_general(
        hidden_act, d_final, contract_rows, preferred_element_type=f32
    ).astype(bf16)
    return (d_head, d_gate, d_up, d_down)


def solution(mesh):
    placed = (
        P("dp", None),
        P("dp", None),
        P("dp", None),
        P("pair", ("dp", "vocab"), None),
        P(),
        P(),
        P(),
        P(None, ("dp", "vocab", "pair")),
        P(None, ("dp", "vocab", "pair")),
        P(("dp", "vocab", "pair"), None),
        P("dp", None),
        P(),
    )
    return jax.shard_map(
        shards,
        mesh=mesh,
        in_specs=placed,
        out_specs=(
            P(("dp", "vocab"), "pair"),
            P(None, ("dp", "vocab", "pair")),
            P(None, ("dp", "vocab", "pair")),
            P(("dp", "vocab", "pair"), None),
        ),
        check_vma=False,
    )
```

```python
import jax
import jax.numpy as jnp
from jax import lax
from jax.sharding import PartitionSpec as P

loss_scale = 256.0
norm_eps = 1e-05
mesh_axes = ("x_hi", "y", "z", "core", "x_lo")

gray = (0, 1, 3, 2)


def moved(block, target, senders=None):
    route = []
    for x in range(4):
        if senders is not None and x not in senders:
            continue
        for y in range(4):
            for z in range(8):
                for c in range(2):
                    tx, ty, tz, tc = target(x, y, z, c)
                    here = (((x // 2) * 4 + y) * 16 + z * 2 + c) * 2 + x % 2
                    there = (((tx // 2) * 4 + ty) * 16 + tz * 2 + tc) * 2 + tx % 2
                    route.append((here, there))
    return lax.ppermute(block, mesh_axes, route)


def along_y(block, distance):
    return moved(block, lambda x, y, z, c: (x, gray[gray[y] ^ distance], z, c))


def along_z(block, distance):
    return moved(block, lambda x, y, z, c: (x, y, z ^ distance, c))


def to_pair(block, senders=None):
    return moved(block, lambda x, y, z, c: (x ^ 1, y, z, c), senders)


def to_outer(block, senders=None):
    return moved(block, lambda x, y, z, c: (3 - x, y, z, c), senders)


def to_opposite(block, senders=None):
    return moved(block, lambda x, y, z, c: (x ^ 2, y, z, c), senders)


def to_core(block):
    return moved(block, lambda x, y, z, c: (x, y, z, c ^ 1))


def after(block, *others):
    return lax.optimization_barrier((block, *others))[0]


def rms_scale(values):
    return lax.rsqrt(jnp.mean(values * values, axis=-1, keepdims=True) + norm_eps)


def normalize(hidden, gain_vector):
    widened = hidden.astype(jnp.float32)
    return (widened * rms_scale(widened) * gain_vector.astype(jnp.float32)).astype(jnp.bfloat16)


def norm_back(hidden, upstream, gain_vector):
    widened = hidden.astype(jnp.float32)
    factor = rms_scale(widened)
    scaled = upstream * gain_vector.astype(jnp.float32)
    inner_sum = jnp.mean(scaled * widened, axis=-1, keepdims=True)
    return (factor * scaled - widened * factor * factor * factor * inner_sum).astype(jnp.bfloat16)


def gathered(own, outer, swap):
    near = [along_y(own, 1), along_y(own, 2)]
    near_outer = [along_y(outer, 1), along_y(outer, 2)]
    half = own.shape[0] // 2
    far = jnp.concatenate([along_y(near[0][:half], 2), along_y(near[1][half:], 1)])
    far_outer = jnp.concatenate([along_y(near_outer[0][:half], 2), along_y(near_outer[1][half:], 1)])
    pieces = []
    for mine, others in ((own, outer), (near[0], near_outer[0]), (near[1], near_outer[1]), (far, far_outer)):
        pieces += [jnp.where(swap, others, mine), jnp.where(swap, mine, others)]
    return jnp.concatenate(pieces)


def to_all(block, axes):
    count = lax.axis_size(axes)
    return lax.all_to_all(jnp.broadcast_to(block, (count, *block.shape)), axes, 0, 0, tiled=True)


def merge(peaks, totals):
    peak = jnp.max(peaks, axis=0)
    return peak, jnp.sum(totals * jnp.exp(peaks - peak), axis=0)


def shards(
    teacher_hidden,
    student_hidden,
    layer_input,
    head,
    teacher_gain,
    student_gain,
    mlp_gain,
    w_gate,
    w_up,
    w_down,
    positions,
    verified,
):
    f32 = jnp.float32
    bf16 = jnp.bfloat16
    x_hi, y, z, c, x_lo = (lax.axis_index(a) for a in mesh_axes)
    is_student = x_lo == 1
    g = y ^ (y >> 1)
    swap = x_hi != (z >> 2)
    width = head.shape[2]
    mask_blk = positions.shape[1]
    half_blk = mask_blk // 2
    group = half_blk // 4
    rows = 8 * half_blk

    head_own = head[0]
    head_other = to_core(head_own)

    step = jnp.arange(half_blk, dtype=jnp.int32)
    order = c * half_blk + ((step // group) ^ (z & 3)) * group + step % group
    picked = positions[0][order]
    raw_teacher, raw_student, raw_input = (
        teacher_hidden[picked],
        student_hidden[picked],
        layer_input[picked],
    )
    own_teacher = normalize(raw_teacher, teacher_gain)
    own_student = normalize(raw_student, student_gain)
    own_rows = jnp.where(is_student, own_student, own_teacher)
    send_rows = jnp.where(is_student, own_teacher, own_student)
    outer_rows = to_outer(send_rows)
    normed = gathered(own_rows, outer_rows, swap)

    contract_width = (((1,), (1,)), ((), ()))
    contract_rows = (((0,), (0,)), ((), ()))
    logits_own = lax.dot_general(
        normed, head_own, contract_width, preferred_element_type=f32
    ).astype(bf16)
    partner_own = to_pair(logits_own)
    logits_side = lax.dot_general(
        normed, head_other, contract_width, preferred_element_type=f32
    ).astype(bf16)
    partner_side = to_pair(logits_side)

    wide_own, wide_side = logits_own.astype(f32), logits_side.astype(f32)
    peak_here = jnp.maximum(
        jnp.max(wide_own, axis=1, keepdims=True), jnp.max(wide_side, axis=1, keepdims=True)
    )
    total_here = jnp.sum(jnp.exp(wide_own - peak_here), axis=1, keepdims=True) + jnp.sum(
        jnp.exp(wide_side - peak_here), axis=1, keepdims=True
    )
    flips = (g * 8 + z) * group
    row_ids = lax.broadcasted_iota(jnp.int32, (rows, rows), 0)
    col_ids = lax.broadcasted_iota(jnp.int32, (rows, rows), 1)
    same_row = (row_ids ^ flips) == col_ids

    def absolute(column):
        return jnp.sum(jnp.where(same_row, column, 0.0), axis=0)

    def relative(line):
        return jnp.sum(jnp.where(same_row, line[None, :], 0.0), axis=1, keepdims=True)

    stats = after(jnp.stack([absolute(peak_here), absolute(total_here)]), partner_own)
    stats = to_all(stats, "z")
    stats = after(jnp.stack(merge(stats[:, 0], stats[:, 1])), partner_side)
    stats = to_all(stats, ("x_hi", "y", "x_lo")).reshape(8, 2, 2, rows)
    peak_teacher, total_teacher = merge(stats[:, 0, 0], stats[:, 0, 1])
    peak_student, total_student = merge(stats[:, 1, 0], stats[:, 1, 1])
    peak_mine = jnp.where(is_student, peak_student, peak_teacher)
    peak_theirs = jnp.where(is_student, peak_teacher, peak_student)
    total_mine = jnp.where(is_student, total_student, total_teacher)
    total_theirs = jnp.where(is_student, total_teacher, total_student)

    flags = verified.astype(f32).reshape(2, 4, 2, half_blk)
    flags = lax.dynamic_index_in_dim(flags, c, 2, keepdims=False)
    flags = jnp.stack([flags[:, gray[i]] for i in range(4)]).reshape(rows)
    sign = jnp.where(is_student, loss_scale, -loss_scale)
    scale = relative(flags * sign)
    peak_mine, total_mine = relative(peak_mine), relative(total_mine)
    peak_theirs, total_theirs = relative(peak_theirs), relative(total_theirs)

    def gradient(mine, theirs):
        probs_mine = jnp.exp(mine.astype(f32) - peak_mine) / total_mine
        probs_theirs = jnp.exp(theirs.astype(f32) - peak_theirs) / total_theirs
        return (scale * (probs_mine - probs_theirs)).astype(bf16)

    grad_own = gradient(logits_own, partner_own)
    grad_side = gradient(logits_side, partner_side)

    partial = jnp.dot(grad_own, head_own, preferred_element_type=f32) + jnp.dot(
        grad_side, head_other, preferred_element_type=f32
    )
    partial = partial.reshape(4, 2, half_blk, width)
    near = along_y(jnp.stack([partial[1, 0], partial[3, 0]]).astype(bf16), 1).astype(f32)
    cross = along_y(jnp.stack([partial[2, 1], partial[3, 1]]).astype(bf16), 2).astype(f32)
    near_next = along_y((partial[2, 0] + near[1]).astype(bf16), 2).astype(f32)
    cross_next = along_y((partial[1, 1] + cross[1]).astype(bf16), 1).astype(f32)
    first = (partial[0, 0] + near[0] + near_next).reshape(4, group, width)
    second = (partial[0, 1] + cross[0] + cross_next).reshape(4, group, width)
    chunks = [first[i] for i in range(4)] + [second[i] for i in range(4)]
    summed = chunks[0]
    for q in range(1, 8):
        summed = summed + along_z(chunks[q].astype(bf16), q).astype(f32)
    students = (1, 3)
    d_normed = (
        jnp.where(is_student, summed, 0.0)
        + to_opposite(summed, students)
        + to_pair(summed, students)
        + to_outer(summed, students)
    )
    raw_here = jnp.where(swap, to_outer(raw_student[:group]), raw_student[:group])
    d_chunk = norm_back(raw_here, d_normed, student_gain)
    d_local = jnp.concatenate([d_chunk] + [along_z(d_chunk, q) for q in range(1, 8)])
    d_near, d_cross = along_y(d_local, 1), along_y(d_local, 2)
    d_far = jnp.concatenate([along_y(d_near[:half_blk], 2), along_y(d_cross[half_blk:], 1)])
    d_pieces = [d_local, d_near, d_cross, d_far]
    d_final = jnp.concatenate(d_pieces + [to_core(piece) for piece in d_pieces])

    own_input = after(normalize(raw_input, mlp_gain), outer_rows)
    outer_input = to_outer(own_input)
    input_here = jnp.concatenate(
        [jnp.where(swap, outer_input, own_input), jnp.where(swap, own_input, outer_input)]
    )
    input_here = after(input_here, logits_side)
    input_near, input_cross = along_y(input_here, 1), along_y(input_here, 2)
    input_near, input_cross, _ = lax.optimization_barrier((input_near, input_cross, grad_own))
    input_far = [along_y(input_near[:half_blk], 2), along_y(input_cross[half_blk:], 1)]
    input_rows = jnp.concatenate([input_here, input_near, input_cross] + input_far)
    normed_input = jnp.concatenate([input_rows, to_core(input_rows)])
    gate_pre = jnp.dot(normed_input, w_gate, preferred_element_type=f32)
    up_pre = jnp.dot(normed_input, w_up, preferred_element_type=f32)
    gate_sigmoid = jax.nn.sigmoid(gate_pre)
    hidden_act = (gate_pre * gate_sigmoid * up_pre).astype(bf16)

    half_width = width // 2
    lent = to_pair(after(normed, partner_side)[:, :half_width], students)
    columns = jnp.where(is_student, normed[:, half_width:], lent)
    columns = jnp.concatenate([columns, to_core(columns)])
    grad_all = jnp.concatenate([grad_own, to_core(grad_side)])
    d_head = lax.dot_general(
        grad_all, columns, contract_rows, preferred_element_type=f32
    ).astype(bf16)

    d_act = lax.dot_general(d_final, w_down, contract_width, preferred_element_type=f32)
    d_gate_pre = (d_act * up_pre * gate_sigmoid * (1.0 + gate_pre * (1.0 - gate_sigmoid))).astype(bf16)
    d_up_pre = (d_act * gate_pre * gate_sigmoid).astype(bf16)
    d_gate = lax.dot_general(
        normed_input, d_gate_pre, contract_rows, preferred_element_type=f32
    ).astype(bf16)
    d_up = lax.dot_general(
        normed_input, d_up_pre, contract_rows, preferred_element_type=f32
    ).astype(bf16)
    d_down = lax.dot_general(
        hidden_act, d_final, contract_rows, preferred_element_type=f32
    ).astype(bf16)
    return (d_head, d_gate, d_up, d_down)


def solution(mesh):
    physical = jax.sharding.Mesh(mesh.devices.reshape(2, 4, 8, 2, 2), mesh_axes)
    by_dp, by_shard = ("x_hi", "y"), ("x_hi", "y", "z", "core")
    placed = (
        P(by_dp, None),
        P(by_dp, None),
        P(by_dp, None),
        P("x_lo", by_shard, None),
        P(),
        P(),
        P(),
        P(None, mesh_axes),
        P(None, mesh_axes),
        P(mesh_axes, None),
        P(by_dp, None),
        P(),
    )
    return jax.shard_map(
        shards,
        mesh=physical,
        in_specs=placed,
        out_specs=(
            P(by_shard, "x_lo"),
            P(None, mesh_axes),
            P(None, mesh_axes),
            P(mesh_axes, None),
        ),
        check_vma=False,
    )
```

```python
import jax
import jax.numpy as jnp
from jax import lax
from jax.experimental import pallas as pl
from jax.experimental.pallas import tpu as pltpu
from jax.sharding import PartitionSpec as P

loss_scale = 256.0
norm_eps = 1e-05
mesh_axes = ("x_hi", "y", "z", "core", "x_lo")

gray = (0, 1, 3, 2)


def moved(block, target, senders=None):
    route = []
    for x in range(4):
        if senders is not None and x not in senders:
            continue
        for y in range(4):
            for z in range(8):
                for c in range(2):
                    tx, ty, tz, tc = target(x, y, z, c)
                    here = (((x // 2) * 4 + y) * 16 + z * 2 + c) * 2 + x % 2
                    there = (((tx // 2) * 4 + ty) * 16 + tz * 2 + tc) * 2 + tx % 2
                    route.append((here, there))
    return lax.ppermute(block, mesh_axes, route)


def along_y(block, distance):
    return moved(block, lambda x, y, z, c: (x, gray[gray[y] ^ distance], z, c))


def along_z(block, distance):
    return moved(block, lambda x, y, z, c: (x, y, z ^ distance, c))


def to_pair(block, senders=None):
    return moved(block, lambda x, y, z, c: (x ^ 1, y, z, c), senders)


def to_outer(block, senders=None):
    return moved(block, lambda x, y, z, c: (3 - x, y, z, c), senders)


def to_opposite(block, senders=None):
    return moved(block, lambda x, y, z, c: (x ^ 2, y, z, c), senders)


def to_core(block):
    return moved(block, lambda x, y, z, c: (x, y, z, c ^ 1))


def after(block, *others):
    return lax.optimization_barrier((block, *others))[0]


def rms_scale(values):
    return lax.rsqrt(jnp.mean(values * values, axis=-1, keepdims=True) + norm_eps)


def normalize(hidden, gain_vector):
    widened = hidden.astype(jnp.float32)
    return (widened * rms_scale(widened) * gain_vector.astype(jnp.float32)).astype(jnp.bfloat16)


def pick_kernel(place, ids, teacher, student, gains, own, send, normed, raw):
    half, group = own.shape[0], own.shape[0] // 4
    f32, bf16 = jnp.float32, jnp.bfloat16
    both_last = (((1,), (1,)), ((), ()))
    spots = lax.broadcasted_iota(jnp.int32, (teacher.shape[0], ids.shape[1]), 0)
    chosen = (spots == ids[...]).astype(f32).astype(bf16)
    row = lax.broadcasted_iota(jnp.int32, (half, ids.shape[1]), 0)
    wanted = place[0] * half + ((row // group) ^ place[2]) * group + row % group
    order = wanted == lax.broadcasted_iota(jnp.int32, (half, ids.shape[1]), 1)
    order = order.astype(f32).astype(bf16)
    chosen = lax.dot_general(order, chosen, both_last, preferred_element_type=f32).astype(bf16)

    def picked(block):
        return jnp.dot(chosen, block[...], preferred_element_type=f32)

    raw_student = picked(student)
    raw_teacher = picked(teacher)
    norm_student = raw_student * rms_scale(raw_student) * gains[1:2].astype(jnp.float32)
    norm_teacher = raw_teacher * rms_scale(raw_teacher) * gains[0:1].astype(jnp.float32)
    is_student = place[1] == 1
    own[...] = jnp.where(is_student, norm_student, norm_teacher).astype(jnp.bfloat16)
    send[...] = jnp.where(is_student, norm_teacher, norm_student).astype(jnp.bfloat16)
    normed[...] = norm_student.astype(jnp.bfloat16)
    raw[...] = raw_student.astype(jnp.bfloat16)


def pick(place, ids, teacher, student, teacher_gain, student_gain):
    operands = (ids, teacher, student, jnp.stack([teacher_gain, student_gain]))
    shape = jax.ShapeDtypeStruct((ids.shape[1] // 2, teacher.shape[1]), jnp.bfloat16)
    whole = [pl.BlockSpec(a.shape, lambda i: (0, 0)) for a in operands]
    return pl.pallas_call(
        pick_kernel,
        grid=(1,),
        in_specs=[pl.BlockSpec(memory_space=pltpu.SMEM)] + whole,
        out_specs=[pl.BlockSpec(shape.shape, lambda i: (0, 0))] * 4,
        out_shape=[shape] * 4,
        compiler_params=pltpu.CompilerParams(vmem_limit_bytes=32 * 2**20),
        name="pick_rows",
    )(place, *operands)


def norm_back(hidden, upstream, gain_vector):
    widened = hidden.astype(jnp.float32)
    factor = rms_scale(widened)
    scaled = upstream * gain_vector.astype(jnp.float32)
    inner_sum = jnp.mean(scaled * widened, axis=-1, keepdims=True)
    return (factor * scaled - widened * factor * factor * factor * inner_sum).astype(jnp.bfloat16)


def gathered(own, outer, swap):
    near = [along_y(own, 1), along_y(own, 2)]
    near_outer = [along_y(outer, 1), along_y(outer, 2)]
    half = own.shape[0] // 2
    far = jnp.concatenate([along_y(near[0][:half], 2), along_y(near[1][half:], 1)])
    far_outer = jnp.concatenate([along_y(near_outer[0][:half], 2), along_y(near_outer[1][half:], 1)])
    pieces = []
    for mine, others in ((own, outer), (near[0], near_outer[0]), (near[1], near_outer[1]), (far, far_outer)):
        pieces += [jnp.where(swap, others, mine), jnp.where(swap, mine, others)]
    return jnp.concatenate(pieces)


def to_all(block, axes):
    count = lax.axis_size(axes)
    return lax.all_to_all(jnp.broadcast_to(block, (count, *block.shape)), axes, 0, 0, tiled=True)


def merge(peaks, totals):
    peak = jnp.max(peaks, axis=0)
    return peak, jnp.sum(totals * jnp.exp(peaks - peak), axis=0)


def shards(
    teacher_hidden,
    student_hidden,
    layer_input,
    head,
    teacher_gain,
    student_gain,
    mlp_gain,
    w_gate,
    w_up,
    w_down,
    positions,
    verified,
):
    f32 = jnp.float32
    bf16 = jnp.bfloat16
    x_hi, y, z, c, x_lo = (lax.axis_index(a) for a in mesh_axes)
    is_student = x_lo == 1
    g = y ^ (y >> 1)
    swap = x_hi != (z >> 2)
    width = head.shape[2]
    mask_blk = positions.shape[1]
    half_blk = mask_blk // 2
    group = half_blk // 4
    rows = 8 * half_blk

    head_own = head[0]
    head_other = to_core(head_own)

    place = jnp.stack([c, x_lo, z & 3]).astype(jnp.int32)
    own_rows, send_rows, own_student, raw_student = pick(
        place, positions, teacher_hidden, student_hidden, teacher_gain, student_gain
    )
    step = jnp.arange(half_blk, dtype=jnp.int32)
    order = c * half_blk + ((step // group) ^ (z & 3)) * group + step % group
    raw_input = layer_input[positions[0][order]]
    outer_rows = to_outer(send_rows)
    normed = gathered(own_rows, outer_rows, swap)

    raw_group = raw_student[:group]
    own_input = after(normalize(raw_input, mlp_gain), outer_rows)
    outer_input = to_outer(jnp.concatenate([own_input, raw_group]))
    raw_here = jnp.where(swap, outer_input[half_blk:], raw_group)
    outer_input = outer_input[:half_blk]
    input_here = jnp.concatenate(
        [jnp.where(swap, outer_input, own_input), jnp.where(swap, own_input, outer_input)]
    )
    input_near, input_cross = along_y(input_here, 1), along_y(input_here, 2)

    contract_width = (((1,), (1,)), ((), ()))
    contract_rows = (((0,), (0,)), ((), ()))
    logits_own = lax.dot_general(
        normed, head_own, contract_width, preferred_element_type=f32
    ).astype(bf16)
    partner_own = to_pair(logits_own)
    logits_side = lax.dot_general(
        normed, head_other, contract_width, preferred_element_type=f32
    ).astype(bf16)
    partner_side = to_pair(logits_side)

    wide_own, wide_side = logits_own.astype(f32), logits_side.astype(f32)
    peak_here = jnp.maximum(
        jnp.max(wide_own, axis=1, keepdims=True), jnp.max(wide_side, axis=1, keepdims=True)
    )
    total_here = jnp.sum(jnp.exp(wide_own - peak_here), axis=1, keepdims=True) + jnp.sum(
        jnp.exp(wide_side - peak_here), axis=1, keepdims=True
    )
    flips = (g * 8 + z) * group
    row_ids = lax.broadcasted_iota(jnp.int32, (rows, rows), 0)
    col_ids = lax.broadcasted_iota(jnp.int32, (rows, rows), 1)
    same_row = (row_ids ^ flips) == col_ids

    def absolute(column):
        return jnp.sum(jnp.where(same_row, column, 0.0), axis=0)

    def relative(line):
        return jnp.sum(jnp.where(same_row, line[None, :], 0.0), axis=1, keepdims=True)

    stats = jnp.stack([absolute(peak_here), absolute(total_here)])
    stats, partner_own, input_near, input_cross = lax.optimization_barrier(
        (stats, partner_own, input_near, input_cross)
    )
    stats = to_all(stats, "z")
    stats = after(jnp.stack(merge(stats[:, 0], stats[:, 1])), partner_side)
    input_near, input_cross, _ = lax.optimization_barrier((input_near, input_cross, stats))
    input_far = [along_y(input_near[:half_blk], 2), along_y(input_cross[half_blk:], 1)]
    stats = to_all(stats, ("x_hi", "y", "x_lo")).reshape(8, 2, 2, rows)
    peak_teacher, total_teacher = merge(stats[:, 0, 0], stats[:, 0, 1])
    peak_student, total_student = merge(stats[:, 1, 0], stats[:, 1, 1])
    peak_mine = jnp.where(is_student, peak_student, peak_teacher)
    peak_theirs = jnp.where(is_student, peak_teacher, peak_student)
    total_mine = jnp.where(is_student, total_student, total_teacher)
    total_theirs = jnp.where(is_student, total_teacher, total_student)

    flags = verified.astype(f32).reshape(2, 4, 2, half_blk)
    flags = lax.dynamic_index_in_dim(flags, c, 2, keepdims=False)
    flags = jnp.stack([flags[:, gray[i]] for i in range(4)]).reshape(rows)
    sign = jnp.where(is_student, loss_scale, -loss_scale)
    scale = relative(flags * sign)
    peak_mine, total_mine = relative(peak_mine), relative(total_mine)
    peak_theirs, total_theirs = relative(peak_theirs), relative(total_theirs)

    def gradient(mine, theirs):
        probs_mine = jnp.exp(mine.astype(f32) - peak_mine) / total_mine
        probs_theirs = jnp.exp(theirs.astype(f32) - peak_theirs) / total_theirs
        return (scale * (probs_mine - probs_theirs)).astype(bf16)

    grad_own = gradient(logits_own, partner_own)
    grad_side = gradient(logits_side, partner_side)

    partial = jnp.dot(grad_own, head_own, preferred_element_type=f32) + jnp.dot(
        grad_side, head_other, preferred_element_type=f32
    )
    partial = partial.reshape(4, 2, half_blk, width)
    near = after(jnp.stack([partial[1, 0], partial[3, 0]]).astype(bf16), *input_far)
    near = along_y(near, 1).astype(f32)
    cross = along_y(jnp.stack([partial[2, 1], partial[3, 1]]).astype(bf16), 2).astype(f32)
    near_next = along_y((partial[2, 0] + near[1]).astype(bf16), 2).astype(f32)
    cross_next = along_y((partial[1, 1] + cross[1]).astype(bf16), 1).astype(f32)
    first = (partial[0, 0] + near[0] + near_next).reshape(4, group, width)
    second = (partial[0, 1] + cross[0] + cross_next).reshape(4, group, width)
    chunks = [first[i] for i in range(4)] + [second[i] for i in range(4)]
    summed = chunks[0]
    for q in range(1, 8):
        summed = summed + along_z(chunks[q].astype(bf16), q).astype(f32)
    summed = summed.astype(bf16)
    students = (1, 3)
    d_normed = (
        jnp.where(is_student, summed, 0.0).astype(f32)
        + to_opposite(summed, students).astype(f32)
        + to_pair(summed, students).astype(f32)
        + to_outer(summed, students).astype(f32)
    )
    d_chunk = norm_back(raw_here, d_normed, student_gain)
    input_rows = jnp.concatenate([input_here, input_near, input_cross] + input_far)
    half_width = width // 2
    lent = to_pair(after(normed, grad_side)[:, :half_width], students)
    columns = jnp.where(is_student, normed[:, half_width:], lent)
    d_chunk, input_side, columns_side, grad_across = lax.optimization_barrier(
        (d_chunk, to_core(input_rows), to_core(columns), to_core(grad_side))
    )
    d_local = jnp.concatenate([d_chunk] + [along_z(d_chunk, q) for q in range(1, 8)])
    d_near, d_cross = along_y(d_local, 1), along_y(d_local, 2)

    normed_input = jnp.concatenate([input_rows, input_side])
    units = w_gate.shape[1]
    pre = jnp.dot(
        normed_input, jnp.concatenate([w_gate, w_up], axis=1), preferred_element_type=f32
    )
    gate_pre, up_pre = pre[:, :units], pre[:, units:]
    gate_sigmoid = jax.nn.sigmoid(gate_pre)
    hidden_act = (gate_pre * gate_sigmoid * up_pre).astype(bf16)
    columns = jnp.concatenate([columns, columns_side])
    grad_all = after(jnp.concatenate([grad_own, grad_across]), d_local)
    d_head = lax.dot_general(
        grad_all, columns, contract_rows, preferred_element_type=f32
    ).astype(bf16)

    d_near, d_cross, hidden_act, d_head = lax.optimization_barrier(
        (d_near, d_cross, hidden_act, d_head)
    )
    d_far = jnp.concatenate([along_y(d_near[:half_blk], 2), along_y(d_cross[half_blk:], 1)])
    d_pieces = [d_local, d_near, d_cross, d_far]
    d_final = jnp.concatenate(d_pieces + [to_core(piece) for piece in d_pieces])

    d_act = lax.dot_general(d_final, w_down, contract_width, preferred_element_type=f32)
    d_gate_pre = (d_act * up_pre * gate_sigmoid * (1.0 + gate_pre * (1.0 - gate_sigmoid))).astype(bf16)
    d_up_pre = (d_act * gate_pre * gate_sigmoid).astype(bf16)
    both = lax.dot_general(
        jnp.concatenate([d_gate_pre, d_up_pre], axis=1),
        normed_input,
        contract_rows,
        preferred_element_type=f32,
    ).astype(bf16)
    d_gate, d_up = both[:units].T, both[units:].T
    d_down = lax.dot_general(
        hidden_act, d_final, contract_rows, preferred_element_type=f32
    ).astype(bf16)
    return (d_head, d_gate, d_up, d_down)


def solution(mesh):
    physical = jax.sharding.Mesh(mesh.devices.reshape(2, 4, 8, 2, 2), mesh_axes)
    by_dp, by_shard = ("x_hi", "y"), ("x_hi", "y", "z", "core")
    placed = (
        P(by_dp, None),
        P(by_dp, None),
        P(by_dp, None),
        P("x_lo", by_shard, None),
        P(),
        P(),
        P(),
        P(None, mesh_axes),
        P(None, mesh_axes),
        P(mesh_axes, None),
        P(by_dp, None),
        P(),
    )
    return jax.shard_map(
        shards,
        mesh=physical,
        in_specs=placed,
        out_specs=(
            P(by_shard, "x_lo"),
            P(None, mesh_axes),
            P(None, mesh_axes),
            P(mesh_axes, None),
        ),
        check_vma=False,
    )
```

```python
import jax
import jax.numpy as jnp
from jax import lax
from jax.experimental import pallas as pl
from jax.experimental.pallas import tpu as pltpu
from jax.sharding import PartitionSpec as P

loss_scale = 256.0
norm_eps = 1e-05
mesh_axes = ("x_hi", "y", "z", "core", "x_lo")

gray = (0, 1, 3, 2)


def moved(block, target, senders=None):
    route = []
    for x in range(4):
        if senders is not None and x not in senders:
            continue
        for y in range(4):
            for z in range(8):
                for c in range(2):
                    tx, ty, tz, tc = target(x, y, z, c)
                    here = (((x // 2) * 4 + y) * 16 + z * 2 + c) * 2 + x % 2
                    there = (((tx // 2) * 4 + ty) * 16 + tz * 2 + tc) * 2 + tx % 2
                    route.append((here, there))
    return lax.ppermute(block, mesh_axes, route)


def along_y(block, distance):
    return moved(block, lambda x, y, z, c: (x, gray[gray[y] ^ distance], z, c))


def along_z(block, distance):
    return moved(block, lambda x, y, z, c: (x, y, z ^ distance, c))


def to_pair(block, senders=None):
    return moved(block, lambda x, y, z, c: (x ^ 1, y, z, c), senders)


def to_outer(block, senders=None):
    return moved(block, lambda x, y, z, c: (3 - x, y, z, c), senders)


def to_opposite(block, senders=None):
    return moved(block, lambda x, y, z, c: (x ^ 2, y, z, c), senders)


def to_core(block):
    return moved(block, lambda x, y, z, c: (x, y, z, c ^ 1))


def after(block, *others):
    return lax.optimization_barrier((block, *others))[0]


def rms_scale(values):
    return lax.rsqrt(jnp.mean(values * values, axis=-1, keepdims=True) + norm_eps)


def normalize(hidden, gain_vector):
    widened = hidden.astype(jnp.float32)
    return (widened * rms_scale(widened) * gain_vector.astype(jnp.float32)).astype(jnp.bfloat16)


def pick_kernel(
    place, ids, teacher, student, teacher_gain, student_gain, own, send, normed, raw
):
    half, group = own.shape[0], own.shape[0] // 4
    f32, bf16 = jnp.float32, jnp.bfloat16
    both_last = (((1,), (1,)), ((), ()))
    spots = lax.broadcasted_iota(jnp.int32, (teacher.shape[0], ids.shape[1]), 0)
    chosen = (spots == ids[...]).astype(f32).astype(bf16)
    row = lax.broadcasted_iota(jnp.int32, (half, ids.shape[1]), 0)
    wanted = place[0] * half + ((row // group) ^ place[2]) * group + row % group
    order = wanted == lax.broadcasted_iota(jnp.int32, (half, ids.shape[1]), 1)
    order = order.astype(f32).astype(bf16)
    chosen = lax.dot_general(order, chosen, both_last, preferred_element_type=f32).astype(bf16)

    def picked(block):
        return jnp.dot(chosen, block[...], preferred_element_type=f32)

    raw_student = picked(student)
    raw_teacher = picked(teacher)
    norm_student = raw_student * rms_scale(raw_student) * student_gain[...].astype(jnp.float32)
    norm_teacher = raw_teacher * rms_scale(raw_teacher) * teacher_gain[...].astype(jnp.float32)
    is_student = place[1] == 1
    own[...] = jnp.where(is_student, norm_student, norm_teacher).astype(jnp.bfloat16)
    send[...] = jnp.where(is_student, norm_teacher, norm_student).astype(jnp.bfloat16)
    normed[...] = norm_student.astype(jnp.bfloat16)
    raw[...] = raw_student.astype(jnp.bfloat16)


def pick(place, ids, teacher, student, teacher_gain, student_gain):
    shape = jax.ShapeDtypeStruct((ids.shape[1] // 2, teacher.shape[1]), jnp.bfloat16)
    operands = (ids, teacher, student, teacher_gain, student_gain)
    whole = [pl.BlockSpec(a.shape, lambda i, rank=a.ndim: (0,) * rank) for a in operands]
    return pl.pallas_call(
        pick_kernel,
        grid=(1,),
        in_specs=[pl.BlockSpec(memory_space=pltpu.SMEM)] + whole,
        out_specs=[pl.BlockSpec(shape.shape, lambda i: (0, 0))] * 4,
        out_shape=[shape] * 4,
        compiler_params=pltpu.CompilerParams(vmem_limit_bytes=56 * 2**20),
        name="pick_rows",
    )(place, *operands)


def norm_back(hidden, upstream, gain_vector):
    widened = hidden.astype(jnp.float32)
    factor = rms_scale(widened)
    scaled = upstream * gain_vector.astype(jnp.float32)
    inner_sum = jnp.mean(scaled * widened, axis=-1, keepdims=True)
    return (factor * scaled - widened * factor * factor * factor * inner_sum).astype(jnp.bfloat16)


def gathered(own, outer, swap):
    near = [along_y(own, 1), along_y(own, 2)]
    near_outer = [along_y(outer, 1), along_y(outer, 2)]
    half = own.shape[0] // 2
    far = jnp.concatenate([along_y(near[0][:half], 2), along_y(near[1][half:], 1)])
    far_outer = jnp.concatenate([along_y(near_outer[0][:half], 2), along_y(near_outer[1][half:], 1)])
    pieces = []
    for mine, others in ((own, outer), (near[0], near_outer[0]), (near[1], near_outer[1]), (far, far_outer)):
        pieces += [jnp.where(swap, others, mine), jnp.where(swap, mine, others)]
    return jnp.concatenate(pieces)


def to_all(block, axes):
    count = lax.axis_size(axes)
    return lax.all_to_all(jnp.broadcast_to(block, (count, *block.shape)), axes, 0, 0, tiled=True)


def merge(peaks, totals):
    peak = jnp.max(peaks, axis=0)
    return peak, jnp.sum(totals * jnp.exp(peaks - peak), axis=0)


def shards(
    teacher_hidden,
    student_hidden,
    layer_input,
    head,
    teacher_gain,
    student_gain,
    mlp_gain,
    w_gate,
    w_up,
    w_down,
    positions,
    verified,
):
    f32 = jnp.float32
    bf16 = jnp.bfloat16
    x_hi, y, z, c, x_lo = (lax.axis_index(a) for a in mesh_axes)
    is_student = x_lo == 1
    g = y ^ (y >> 1)
    swap = x_hi != (z >> 2)
    width = head.shape[2]
    mask_blk = positions.shape[1]
    half_blk = mask_blk // 2
    group = half_blk // 4
    rows = 8 * half_blk

    head_own = head[0]
    head_other = to_core(head_own)

    place = jnp.stack([c, x_lo, z & 3]).astype(jnp.int32)
    own_rows, send_rows, own_student, raw_student = pick(
        place, positions, teacher_hidden, student_hidden, teacher_gain, student_gain
    )
    step = jnp.arange(half_blk, dtype=jnp.int32)
    order = c * half_blk + ((step // group) ^ (z & 3)) * group + step % group
    raw_input = layer_input[positions[0][order]]
    outer_rows = to_outer(send_rows)
    normed = gathered(own_rows, outer_rows, swap)

    raw_group = raw_student[:group]
    own_input = after(normalize(raw_input, mlp_gain), outer_rows)
    outer_input = to_outer(jnp.concatenate([own_input, raw_group]))
    raw_here = jnp.where(swap, outer_input[half_blk:], raw_group)
    outer_input = outer_input[:half_blk]
    input_here = jnp.concatenate(
        [jnp.where(swap, outer_input, own_input), jnp.where(swap, own_input, outer_input)]
    )
    input_near, input_cross = along_y(input_here, 1), along_y(input_here, 2)

    contract_width = (((1,), (1,)), ((), ()))
    contract_rows = (((0,), (0,)), ((), ()))
    logits_own = lax.dot_general(
        normed, head_own, contract_width, preferred_element_type=f32
    ).astype(bf16)
    partner_own = to_pair(logits_own)
    logits_side = lax.dot_general(
        normed, head_other, contract_width, preferred_element_type=f32
    ).astype(bf16)
    partner_side = to_pair(logits_side)

    wide_own, wide_side = logits_own.astype(f32), logits_side.astype(f32)
    peak_here = jnp.maximum(
        jnp.max(wide_own, axis=1, keepdims=True), jnp.max(wide_side, axis=1, keepdims=True)
    )
    total_here = jnp.sum(jnp.exp(wide_own - peak_here), axis=1, keepdims=True) + jnp.sum(
        jnp.exp(wide_side - peak_here), axis=1, keepdims=True
    )
    flips = (g * 8 + z) * group
    row_ids = lax.broadcasted_iota(jnp.int32, (rows, rows), 0)
    col_ids = lax.broadcasted_iota(jnp.int32, (rows, rows), 1)
    same_row = (row_ids ^ flips) == col_ids

    def absolute(column):
        return jnp.sum(jnp.where(same_row, column, 0.0), axis=0)

    def relative(line):
        return jnp.sum(jnp.where(same_row, line[None, :], 0.0), axis=1, keepdims=True)

    stats = jnp.stack([absolute(peak_here), absolute(total_here)])
    stats, partner_own, input_near, input_cross = lax.optimization_barrier(
        (stats, partner_own, input_near, input_cross)
    )
    stats = to_all(stats, "z")
    stats = after(jnp.stack(merge(stats[:, 0], stats[:, 1])), partner_side)
    input_near, input_cross, _ = lax.optimization_barrier((input_near, input_cross, stats))
    input_far = [along_y(input_near[:half_blk], 2), along_y(input_cross[half_blk:], 1)]
    stats = to_all(stats, ("x_hi", "y", "x_lo")).reshape(8, 2, 2, rows)
    peak_teacher, total_teacher = merge(stats[:, 0, 0], stats[:, 0, 1])
    peak_student, total_student = merge(stats[:, 1, 0], stats[:, 1, 1])
    peak_mine = jnp.where(is_student, peak_student, peak_teacher)
    peak_theirs = jnp.where(is_student, peak_teacher, peak_student)
    total_mine = jnp.where(is_student, total_student, total_teacher)
    total_theirs = jnp.where(is_student, total_teacher, total_student)

    flags = verified.astype(f32).reshape(2, 4, 2, half_blk)
    flags = lax.dynamic_index_in_dim(flags, c, 2, keepdims=False)
    flags = jnp.stack([flags[:, gray[i]] for i in range(4)]).reshape(rows)
    sign = jnp.where(is_student, loss_scale, -loss_scale)
    scale = relative(flags * sign)
    peak_mine, total_mine = relative(peak_mine), relative(total_mine)
    peak_theirs, total_theirs = relative(peak_theirs), relative(total_theirs)

    def gradient(mine, theirs):
        probs_mine = jnp.exp(mine.astype(f32) - peak_mine) / total_mine
        probs_theirs = jnp.exp(theirs.astype(f32) - peak_theirs) / total_theirs
        return (scale * (probs_mine - probs_theirs)).astype(bf16)

    grad_own = gradient(logits_own, partner_own)
    grad_side = gradient(logits_side, partner_side)

    partial = jnp.dot(grad_own, head_own, preferred_element_type=f32) + jnp.dot(
        grad_side, head_other, preferred_element_type=f32
    )
    partial = partial.reshape(4, 2, half_blk, width)
    near = after(jnp.stack([partial[1, 0], partial[3, 0]]).astype(bf16), *input_far)
    near = along_y(near, 1).astype(f32)
    cross = along_y(jnp.stack([partial[2, 1], partial[3, 1]]).astype(bf16), 2).astype(f32)
    near_next = along_y((partial[2, 0] + near[1]).astype(bf16), 2).astype(f32)
    cross_next = along_y((partial[1, 1] + cross[1]).astype(bf16), 1).astype(f32)
    first = (partial[0, 0] + near[0] + near_next).reshape(4, group, width)
    second = (partial[0, 1] + cross[0] + cross_next).reshape(4, group, width)
    chunks = [first[i] for i in range(4)] + [second[i] for i in range(4)]
    summed = chunks[0]
    for q in range(1, 8):
        summed = summed + along_z(chunks[q].astype(bf16), q).astype(f32)
    summed = summed.astype(bf16)
    students = (1, 3)
    d_normed = (
        jnp.where(is_student, summed, 0.0).astype(f32)
        + to_opposite(summed, students).astype(f32)
        + to_pair(summed, students).astype(f32)
        + to_outer(summed, students).astype(f32)
    )
    d_chunk = norm_back(raw_here, d_normed, student_gain)
    input_rows = jnp.concatenate([input_here, input_near, input_cross] + input_far)
    half_width = width // 2
    lent = to_pair(after(normed, grad_side)[:, :half_width], students)
    columns = jnp.where(is_student, normed[:, half_width:], lent)
    d_chunk, input_side, columns_side, grad_across = lax.optimization_barrier(
        (d_chunk, to_core(input_rows), to_core(columns), to_core(grad_side))
    )
    d_local = jnp.concatenate([d_chunk] + [along_z(d_chunk, q) for q in range(1, 8)])
    d_near, d_cross = along_y(d_local, 1), along_y(d_local, 2)

    normed_input = jnp.concatenate([input_rows, after(input_side, d_local)])
    units = w_gate.shape[1]
    pre = jnp.dot(
        normed_input, jnp.concatenate([w_gate, w_up], axis=1), preferred_element_type=f32
    )
    gate_pre, up_pre = pre[:, :units], pre[:, units:]
    gate_sigmoid = jax.nn.sigmoid(gate_pre)
    hidden_act = (gate_pre * gate_sigmoid * up_pre).astype(bf16)
    columns = jnp.concatenate([columns, columns_side])
    grad_all = after(jnp.concatenate([grad_own, grad_across]), d_local)
    d_head = lax.dot_general(
        grad_all, columns, contract_rows, preferred_element_type=f32
    ).astype(bf16)

    d_near, d_cross, hidden_act, d_head = lax.optimization_barrier(
        (d_near, d_cross, hidden_act, d_head)
    )
    d_far = jnp.concatenate([along_y(d_near[:half_blk], 2), along_y(d_cross[half_blk:], 1)])
    d_pieces = [d_local, d_near, d_cross, d_far]
    d_final = jnp.concatenate(d_pieces + [to_core(piece) for piece in d_pieces])

    d_act = lax.dot_general(d_final, w_down, contract_width, preferred_element_type=f32)
    d_gate_pre = (d_act * up_pre * gate_sigmoid * (1.0 + gate_pre * (1.0 - gate_sigmoid))).astype(bf16)
    d_up_pre = (d_act * gate_pre * gate_sigmoid).astype(bf16)
    both = lax.dot_general(
        jnp.concatenate([d_gate_pre, d_up_pre], axis=1),
        normed_input,
        contract_rows,
        preferred_element_type=f32,
    ).astype(bf16)
    d_gate, d_up = both[:units].T, both[units:].T
    d_down = lax.dot_general(
        hidden_act, d_final, contract_rows, preferred_element_type=f32
    ).astype(bf16)
    return (d_head, d_gate, d_up, d_down)


def solution(mesh):
    physical = jax.sharding.Mesh(mesh.devices.reshape(2, 4, 8, 2, 2), mesh_axes)
    by_dp, by_shard = ("x_hi", "y"), ("x_hi", "y", "z", "core")
    placed = (
        P(by_dp, None),
        P(by_dp, None),
        P(by_dp, None),
        P("x_lo", by_shard, None),
        P(),
        P(),
        P(),
        P(None, mesh_axes),
        P(None, mesh_axes),
        P(mesh_axes, None),
        P(by_dp, None),
        P(),
    )
    return jax.shard_map(
        shards,
        mesh=physical,
        in_specs=placed,
        out_specs=(
            P(by_shard, "x_lo"),
            P(None, mesh_axes),
            P(None, mesh_axes),
            P(mesh_axes, None),
        ),
        check_vma=False,
    )
```

```python
import jax
import jax.numpy as jnp
from jax import lax
from jax.experimental import pallas as pl
from jax.experimental.pallas import tpu as pltpu
from jax.sharding import PartitionSpec as P

loss_scale = 256.0
norm_eps = 1e-05
mesh_axes = ("x_hi", "y", "z", "core", "x_lo")

gray = (0, 1, 3, 2)


def moved(block, target, senders=None):
    route = []
    for x in range(4):
        if senders is not None and x not in senders:
            continue
        for y in range(4):
            for z in range(8):
                for c in range(2):
                    tx, ty, tz, tc = target(x, y, z, c)
                    here = (((x // 2) * 4 + y) * 16 + z * 2 + c) * 2 + x % 2
                    there = (((tx // 2) * 4 + ty) * 16 + tz * 2 + tc) * 2 + tx % 2
                    route.append((here, there))
    return lax.ppermute(block, mesh_axes, route)


def along_y(block, distance):
    return moved(block, lambda x, y, z, c: (x, gray[gray[y] ^ distance], z, c))


def along_z(block, distance):
    return moved(block, lambda x, y, z, c: (x, y, z ^ distance, c))


def to_pair(block, senders=None):
    return moved(block, lambda x, y, z, c: (x ^ 1, y, z, c), senders)


def to_outer(block, senders=None):
    return moved(block, lambda x, y, z, c: (3 - x, y, z, c), senders)


def to_opposite(block, senders=None):
    return moved(block, lambda x, y, z, c: (x ^ 2, y, z, c), senders)


def to_core(block):
    return moved(block, lambda x, y, z, c: (x, y, z, c ^ 1))


def after(block, *others):
    return lax.optimization_barrier((block, *others))[0]


def rms_scale(values):
    return lax.rsqrt(jnp.mean(values * values, axis=-1, keepdims=True) + norm_eps)


def normalize(hidden, gain_vector):
    widened = hidden.astype(jnp.float32)
    return (widened * rms_scale(widened) * gain_vector.astype(jnp.float32)).astype(jnp.bfloat16)


def pick_kernel(
    place, ids, teacher, student, teacher_gain, student_gain, own, send, normed, raw
):
    half, group = own.shape[0], own.shape[0] // 4
    f32, bf16 = jnp.float32, jnp.bfloat16
    both_last = (((1,), (1,)), ((), ()))
    spots = lax.broadcasted_iota(jnp.int32, (teacher.shape[0], ids.shape[1]), 0)
    chosen = (spots == ids[...]).astype(f32).astype(bf16)
    row = lax.broadcasted_iota(jnp.int32, (half, ids.shape[1]), 0)
    wanted = place[0] * half + ((row // group) ^ place[2]) * group + row % group
    order = wanted == lax.broadcasted_iota(jnp.int32, (half, ids.shape[1]), 1)
    order = order.astype(f32).astype(bf16)
    chosen = lax.dot_general(order, chosen, both_last, preferred_element_type=f32).astype(bf16)

    def picked(block):
        return jnp.dot(chosen, block[...], preferred_element_type=f32)

    raw_student = picked(student)
    raw_teacher = picked(teacher)
    norm_student = raw_student * rms_scale(raw_student) * student_gain[...].astype(jnp.float32)
    norm_teacher = raw_teacher * rms_scale(raw_teacher) * teacher_gain[...].astype(jnp.float32)
    is_student = place[1] == 1
    own[...] = jnp.where(is_student, norm_student, norm_teacher).astype(jnp.bfloat16)
    send[...] = jnp.where(is_student, norm_teacher, norm_student).astype(jnp.bfloat16)
    normed[...] = norm_student.astype(jnp.bfloat16)
    raw[...] = raw_student.astype(jnp.bfloat16)


def pick(place, ids, teacher, student, teacher_gain, student_gain):
    shape = jax.ShapeDtypeStruct((ids.shape[1] // 2, teacher.shape[1]), jnp.bfloat16)
    operands = (ids, teacher, student, teacher_gain, student_gain)
    whole = [pl.BlockSpec(a.shape, lambda i, rank=a.ndim: (0,) * rank) for a in operands]
    return pl.pallas_call(
        pick_kernel,
        grid=(1,),
        in_specs=[pl.BlockSpec(memory_space=pltpu.SMEM)] + whole,
        out_specs=[pl.BlockSpec(shape.shape, lambda i: (0, 0))] * 4,
        out_shape=[shape] * 4,
        compiler_params=pltpu.CompilerParams(vmem_limit_bytes=56 * 2**20),
        name="pick_rows",
    )(place, *operands)


def norm_back(hidden, upstream, gain_vector):
    widened = hidden.astype(jnp.float32)
    factor = rms_scale(widened)
    scaled = upstream * gain_vector.astype(jnp.float32)
    inner_sum = jnp.mean(scaled * widened, axis=-1, keepdims=True)
    return (factor * scaled - widened * factor * factor * factor * inner_sum).astype(jnp.bfloat16)


def gathered(own, outer, swap):
    near = [along_y(own, 1), along_y(own, 2)]
    near_outer = [along_y(outer, 1), along_y(outer, 2)]
    half = own.shape[0] // 2
    far = jnp.concatenate([along_y(near[0][:half], 2), along_y(near[1][half:], 1)])
    far_outer = jnp.concatenate([along_y(near_outer[0][:half], 2), along_y(near_outer[1][half:], 1)])
    pieces = []
    for mine, others in ((own, outer), (near[0], near_outer[0]), (near[1], near_outer[1]), (far, far_outer)):
        pieces += [jnp.where(swap, others, mine), jnp.where(swap, mine, others)]
    return jnp.concatenate(pieces)


def to_all(block, axes):
    count = lax.axis_size(axes)
    return lax.all_to_all(jnp.broadcast_to(block, (count, *block.shape)), axes, 0, 0, tiled=True)


def merge(peaks, totals):
    peak = jnp.max(peaks, axis=0)
    return peak, jnp.sum(totals * jnp.exp(peaks - peak), axis=0)


def shards(
    teacher_hidden,
    student_hidden,
    layer_input,
    head,
    teacher_gain,
    student_gain,
    mlp_gain,
    w_gate,
    w_up,
    w_down,
    positions,
    verified,
):
    f32 = jnp.float32
    bf16 = jnp.bfloat16
    x_hi, y, z, c, x_lo = (lax.axis_index(a) for a in mesh_axes)
    is_student = x_lo == 1
    g = y ^ (y >> 1)
    swap = x_hi != (z >> 2)
    width = head.shape[2]
    mask_blk = positions.shape[1]
    half_blk = mask_blk // 2
    group = half_blk // 4
    rows = 8 * half_blk

    head_own = head[0]
    head_other = to_core(head_own)

    place = jnp.stack([c, x_lo, z & 3]).astype(jnp.int32)
    own_rows, send_rows, own_student, raw_student = pick(
        place, positions, teacher_hidden, student_hidden, teacher_gain, student_gain
    )
    step = jnp.arange(half_blk, dtype=jnp.int32)
    order = c * half_blk + ((step // group) ^ (z & 3)) * group + step % group
    raw_input = layer_input[positions[0][order]]
    outer_rows = to_outer(send_rows)
    normed = gathered(own_rows, outer_rows, swap)

    raw_group = raw_student[:group]
    own_input = after(normalize(raw_input, mlp_gain), outer_rows)
    outer_input = to_outer(jnp.concatenate([own_input, raw_group]))
    raw_here = jnp.where(swap, outer_input[half_blk:], raw_group)
    outer_input = outer_input[:half_blk]
    input_here = jnp.concatenate(
        [jnp.where(swap, outer_input, own_input), jnp.where(swap, own_input, outer_input)]
    )
    input_near, input_cross = along_y(input_here, 1), along_y(input_here, 2)

    contract_width = (((1,), (1,)), ((), ()))
    contract_rows = (((0,), (0,)), ((), ()))
    logits_own = lax.dot_general(
        normed, head_own, contract_width, preferred_element_type=f32
    ).astype(bf16)
    partner_own = to_pair(logits_own)
    logits_side = lax.dot_general(
        normed, head_other, contract_width, preferred_element_type=f32
    ).astype(bf16)
    partner_side = to_pair(logits_side)

    wide_own, wide_side = logits_own.astype(f32), logits_side.astype(f32)
    peak_here = jnp.maximum(
        jnp.max(wide_own, axis=1, keepdims=True), jnp.max(wide_side, axis=1, keepdims=True)
    )
    total_here = jnp.sum(jnp.exp(wide_own - peak_here), axis=1, keepdims=True) + jnp.sum(
        jnp.exp(wide_side - peak_here), axis=1, keepdims=True
    )
    flips = (g * 8 + z) * group
    row_ids = lax.broadcasted_iota(jnp.int32, (rows, rows), 0)
    col_ids = lax.broadcasted_iota(jnp.int32, (rows, rows), 1)
    same_row = (row_ids ^ flips) == col_ids

    def absolute(column):
        return jnp.sum(jnp.where(same_row, column, 0.0), axis=0)

    def relative(line):
        return jnp.sum(jnp.where(same_row, line[None, :], 0.0), axis=1, keepdims=True)

    stats = jnp.stack([absolute(peak_here), absolute(total_here)])
    stats, partner_own, input_near, input_cross = lax.optimization_barrier(
        (stats, partner_own, input_near, input_cross)
    )
    stats = to_all(stats, "z")
    stats = jnp.stack(merge(stats[:, 0], stats[:, 1]))
    input_near, input_cross, _ = lax.optimization_barrier((input_near, input_cross, stats))
    input_far = [along_y(input_near[:half_blk], 2), along_y(input_cross[half_blk:], 1)]
    stats = to_all(stats, ("x_hi", "y", "x_lo")).reshape(8, 2, 2, rows)
    peak_teacher, total_teacher = merge(stats[:, 0, 0], stats[:, 0, 1])
    peak_student, total_student = merge(stats[:, 1, 0], stats[:, 1, 1])
    peak_mine = jnp.where(is_student, peak_student, peak_teacher)
    peak_theirs = jnp.where(is_student, peak_teacher, peak_student)
    total_mine = jnp.where(is_student, total_student, total_teacher)
    total_theirs = jnp.where(is_student, total_teacher, total_student)

    flags = verified.astype(f32).reshape(2, 4, 2, half_blk)
    flags = lax.dynamic_index_in_dim(flags, c, 2, keepdims=False)
    flags = jnp.stack([flags[:, gray[i]] for i in range(4)]).reshape(rows)
    sign = jnp.where(is_student, loss_scale, -loss_scale)
    scale = relative(flags * sign)
    peak_mine, total_mine = relative(peak_mine), relative(total_mine)
    peak_theirs, total_theirs = relative(peak_theirs), relative(total_theirs)

    def gradient(mine, theirs):
        probs_mine = jnp.exp(mine.astype(f32) - peak_mine) / total_mine
        probs_theirs = jnp.exp(theirs.astype(f32) - peak_theirs) / total_theirs
        return (scale * (probs_mine - probs_theirs)).astype(bf16)

    grad_own = gradient(logits_own, partner_own)
    grad_side = gradient(logits_side, partner_side)

    partial = jnp.dot(grad_own, head_own, preferred_element_type=f32) + jnp.dot(
        grad_side, head_other, preferred_element_type=f32
    )
    partial = partial.reshape(4, 2, half_blk, width)
    near = after(jnp.stack([partial[1, 0], partial[3, 0]]).astype(bf16), *input_far)
    near = along_y(near, 1).astype(f32)
    cross = along_y(jnp.stack([partial[2, 1], partial[3, 1]]).astype(bf16), 2).astype(f32)
    near_next = along_y((partial[2, 0] + near[1]).astype(bf16), 2).astype(f32)
    cross_next = along_y((partial[1, 1] + cross[1]).astype(bf16), 1).astype(f32)
    first = (partial[0, 0] + near[0] + near_next).reshape(4, group, width)
    second = (partial[0, 1] + cross[0] + cross_next).reshape(4, group, width)
    chunks = [first[i] for i in range(4)] + [second[i] for i in range(4)]
    summed = chunks[0]
    for q in range(1, 8):
        summed = summed + along_z(chunks[q].astype(bf16), q).astype(f32)
    summed = summed.astype(bf16)
    students = (1, 3)
    d_normed = (
        jnp.where(is_student, summed, 0.0).astype(f32)
        + to_opposite(summed, students).astype(f32)
        + to_pair(summed, students).astype(f32)
        + to_outer(summed, students).astype(f32)
    )
    d_chunk = norm_back(raw_here, d_normed, student_gain)
    input_rows = jnp.concatenate([input_here, input_near, input_cross] + input_far)
    half_width = width // 2
    lent = to_pair(after(normed, grad_side)[:, :half_width], students)
    columns = jnp.where(is_student, normed[:, half_width:], lent)
    d_chunk, input_side, columns_side, grad_across = lax.optimization_barrier(
        (d_chunk, to_core(input_rows), to_core(columns), to_core(grad_side))
    )
    d_local = jnp.concatenate([d_chunk] + [along_z(d_chunk, q) for q in range(1, 8)])
    d_near, d_cross = along_y(d_local, 1), along_y(d_local, 2)

    normed_input = jnp.concatenate([input_rows, after(input_side, d_local)])
    units = w_gate.shape[1]
    pre = jnp.dot(
        normed_input, jnp.concatenate([w_gate, w_up], axis=1), preferred_element_type=f32
    )
    gate_pre, up_pre = pre[:, :units], pre[:, units:]
    gate_sigmoid = jax.nn.sigmoid(gate_pre)
    hidden_act = (gate_pre * gate_sigmoid * up_pre).astype(bf16)
    columns = jnp.concatenate([columns, columns_side])
    grad_all = after(jnp.concatenate([grad_own, grad_across]), d_local)
    d_head = lax.dot_general(
        grad_all, columns, contract_rows, preferred_element_type=f32
    ).astype(bf16)

    d_near, d_cross, hidden_act, d_head = lax.optimization_barrier(
        (d_near, d_cross, hidden_act, d_head)
    )
    d_far = jnp.concatenate([along_y(d_near[:half_blk], 2), along_y(d_cross[half_blk:], 1)])
    d_pieces = [d_local, d_near, d_cross, d_far]
    d_final = jnp.concatenate(d_pieces + [to_core(piece) for piece in d_pieces])

    d_act = lax.dot_general(d_final, w_down, contract_width, preferred_element_type=f32)
    d_gate_pre = (d_act * up_pre * gate_sigmoid * (1.0 + gate_pre * (1.0 - gate_sigmoid))).astype(bf16)
    d_up_pre = (d_act * gate_pre * gate_sigmoid).astype(bf16)
    both = lax.dot_general(
        jnp.concatenate([d_gate_pre, d_up_pre], axis=1),
        normed_input,
        contract_rows,
        preferred_element_type=f32,
    ).astype(bf16)
    d_gate, d_up = both[:units].T, both[units:].T
    d_down = lax.dot_general(
        hidden_act, d_final, contract_rows, preferred_element_type=f32
    ).astype(bf16)
    return (d_head, d_gate, d_up, d_down)


def solution(mesh):
    physical = jax.sharding.Mesh(mesh.devices.reshape(2, 4, 8, 2, 2), mesh_axes)
    by_dp, by_shard = ("x_hi", "y"), ("x_hi", "y", "z", "core")
    placed = (
        P(by_dp, None),
        P(by_dp, None),
        P(by_dp, None),
        P("x_lo", by_shard, None),
        P(),
        P(),
        P(),
        P(None, mesh_axes),
        P(None, mesh_axes),
        P(mesh_axes, None),
        P(by_dp, None),
        P(),
    )
    return jax.shard_map(
        shards,
        mesh=physical,
        in_specs=placed,
        out_specs=(
            P(by_shard, "x_lo"),
            P(None, mesh_axes),
            P(None, mesh_axes),
            P(mesh_axes, None),
        ),
        check_vma=False,
    )
```
